256 devices in a mesh: tm: 16 (over y_lo, x, core), space: 16 (over y_hi, z).
Axes of the slice: x: 4, y: 4 (y_hi: 2, y_lo: 2; y = y_hi * 2 + y_lo), z: 8, core: 2. Of those that a mesh axis runs over, the one named last changes fastest.
Arguments:
- eigvecs: bfloat16 [2, 64, 21504, 256], P(None, 'tm', 'space'), may hold values from -0.03125 to 0.03125
- solutions: bfloat16 [2, 64, 21504, 256], P(None, 'tm', 'space'), may hold values from -6 to 6
- elementals: bfloat16 [2, 64, 256, 256], P(None, 'tm'), may hold values from -0.25 to 0.25
- source_list: int32 [4], replicated, may hold values from 0 to 63
- pair_owner: int32 [16, 16], replicated, may hold values from 0 to 15, each once within a row
- dilution_order: int32 [64], replicated, may hold values from 0 to 63, each once
Outputs:
- boxes: bfloat16 [256, 2, 256, 256], P('tm', None, 'space')
The draws below stay inside these ranges and needn't reach their ends.
Inputs may be any that keep to these rules, and one draw needn't show every extreme that they name: `pair_owner`: each row is a permutation of the tm indices. `dilution_order`: a permutation of the dilution columns.
All inputs are finite; a program needn't handle non-finite values.
Results may differ from the reference program's by a relative error of at most 0.0064.
Values may be sent and summed in bfloat16 or wider, within the bound.
No kernel may reach another device: no remote copies, remote signals or barrier semaphores. Data moves between devices by JAX's collectives and lax.ppermute only.
A program may use at most 64 MiB of HBM per device.

```python
import jax
import jax.numpy as jnp
from jax import lax

NEV = 256
NCOL = 64
SPINS = 4
SC = 256
NT = 64
NSRC = 4
KROWS = 21504
N_TM = 16


def touch_ends(values, own_key, low, largest):
    dims = values.shape
    spot = [jax.random.randint(jax.random.fold_in(own_key, axis), (), 0, dims[axis]) for axis in range(len(dims))]
    values = values.at[tuple(spot)].set(low)
    longest = dims.index(max(dims))
    spot[longest] = (spot[longest] + 1) % dims[longest]
    return values.at[tuple(spot)].set(largest)


def shard_levels(rng, dims, shards, low, high):
    level, own = 1.0, jax.random.fold_in(rng, 6)
    for axis_at, parts in shards:
        steps = jnp.exp(jax.random.uniform(jax.random.fold_in(own, axis_at), (parts,), jnp.float32, low / len(shards), high / len(shards)))
        level = level * jnp.repeat(steps, dims[axis_at] // parts).reshape([-1 if axis == axis_at else 1 for axis in range(len(dims))])
    return level


def noise(key, shape, spread, reach, split=(), dtype=jnp.bfloat16):
    loudness = shard_levels(key, shape, split, -0.22, 0.18) if split else 1.0
    entries = jax.random.normal(key, shape, jnp.float32) * spread * loudness
    return jnp.minimum(jnp.maximum(entries, -reach), reach).astype(dtype)


def setup_inputs(seed: int = 0) -> dict:
    splits = jax.random.split(jax.random.key(seed), 7)
    return {
        "eigvecs": noise(splits[0], (2, NT, KROWS, NEV), (2 * KROWS) ** -0.5, 0.03125, ((1, 16), (2, 16))),
        "solutions": noise(splits[1], (2, NT, KROWS, SC), 1.0, 6.0, ((1, 16), (2, 16))),
        "elementals": noise(splits[2], (2, NT, NEV, NEV), (2 * NEV) ** -0.5, 0.25, ((1, 16),)),
        "source_list": touch_ends(jax.random.randint(splits[3], (NSRC,), 0, NT), jax.random.fold_in(splits[3], 1), 0, NT - 1).astype(jnp.int32),
        "pair_owner": jax.vmap(lambda own: jax.random.permutation(own, N_TM))(jax.random.split(splits[4], N_TM)).reshape((N_TM, N_TM)).astype(jnp.int32),
        "dilution_order": jax.random.permutation(splits[5], NCOL).astype(jnp.int32),
    }


def conj_product(left, right, form):
    left = left.astype(jnp.float32)
    right = right.astype(jnp.float32)
    real_part = jnp.einsum(form, left[0], right[0]) + jnp.einsum(form, left[1], right[1])
    imag_part = jnp.einsum(form, left[0], right[1]) - jnp.einsum(form, left[1], right[0])
    return jnp.stack([real_part, imag_part])


def reference(eigvecs, solutions, elementals, source_list, pair_owner, dilution_order):
    def project(slice_number):
        vectors = lax.dynamic_index_in_dim(eigvecs, slice_number, 1, keepdims=False)
        columns = lax.dynamic_index_in_dim(solutions, slice_number, 1, keepdims=False)
        return conj_product(vectors, columns, "km,kn->mn").astype(jnp.bfloat16)

    projected = lax.map(project, jnp.arange(NT).astype(jnp.int32))
    projected_t = jnp.transpose(projected, (1, 0, 2, 3))
    weighted = conj_product(elementals, projected_t, "tkm,tkn->tmn").astype(jnp.bfloat16)
    sources = projected[source_list]
    sources = sources.reshape(NSRC, 2, NEV, SPINS, NCOL)[..., dilution_order]
    sources = jnp.transpose(sources.reshape(NSRC, 2, NEV, SC), (1, 0, 2, 3))
    scale = (2.0 * NEV) ** -0.5
    tiles = (conj_product(weighted, sources, "tkm,skn->tsmn") * scale).astype(jnp.bfloat16)
    tiles = jnp.transpose(tiles, (1, 2, 0, 3, 4)).reshape(NT * NSRC, 2, SC, SC)
    senders = jnp.broadcast_to(jnp.arange(N_TM).astype(jnp.int32)[:, None], (N_TM, N_TM))
    slots = jnp.broadcast_to(jnp.arange(N_TM).astype(jnp.int32)[None, :], (N_TM, N_TM))
    inverse = jnp.zeros((N_TM, N_TM), jnp.int32).at[senders, pair_owner].set(slots)
    order = jnp.transpose(senders * N_TM + inverse).reshape(-1)
    return tiles[order]
```

```python
import functools

import jax
import jax.numpy as jnp
from jax import lax
from jax.experimental import pallas as pl
from jax.experimental.pallas import tpu as pltpu
from jax.sharding import Mesh
from jax.sharding import PartitionSpec as P

TM = ("yl", "x", "core")
SPACE = ("yh", "z")
TD = 4
HALF = 2
NS = 4
NEV = 256
SC = 256
WIDTH = 16
SPINS = 4
F32 = jnp.float32
BF16 = jnp.bfloat16


def any_space():
    return pl.BlockSpec(memory_space=pl.ANY)


def smem():
    return pl.BlockSpec(memory_space=pltpu.SMEM)


def slot_timeslices(src, group):
    flags = []
    for t in range(TD):
        hit = src(0) == group * TD + t
        for s in range(1, NS):
            hit = jnp.logical_or(hit, src(s) == group * TD + t)
        flags.append(hit.astype(jnp.int32))
    total = flags[0] + flags[1] + flags[2] + flags[3]
    slots = []
    before = jnp.int32(0)
    for t in range(TD):
        slots.append(jnp.where(flags[t] == 1, before, total + t - before))
        before = before + flags[t]
    return slots


def slot_of(slots, t):
    out = slots[0]
    for k in range(1, TD):
        out = jnp.where(t == k, slots[k], out)
    return out


def timeslice_at(slots, place):
    out = jnp.int32(0)
    for t in range(1, TD):
        out = jnp.where(slots[t] == place, t, out)
    return out


def project_kernel(src_ref, group_ref, vec_ref, sol_ref, out_ref, acc_ref):
    del src_ref, group_ref
    kb = pl.program_id(1)
    depth = vec_ref.shape[2]
    vec = vec_ref[...].reshape(2, depth, NEV)
    sol = sol_ref[...].reshape(2 * depth, SC)
    straight = vec.reshape(2 * depth, NEV)
    turned = jnp.concatenate([-vec[1], vec[0]], axis=0)
    dims = (((0,), (0,)), ((), ()))
    real = lax.dot_general(sol, straight, dims, preferred_element_type=F32)
    imag = lax.dot_general(sol, turned, dims, preferred_element_type=F32)

    @pl.when(kb == 0)
    def _():
        acc_ref[0] = real
        acc_ref[1] = imag

    @pl.when(kb > 0)
    def _():
        acc_ref[0] += real
        acc_ref[1] += imag

    @pl.when(kb == pl.num_programs(1) - 1)
    def _():
        for part in range(2):
            out_ref[:, 0, part] = acc_ref[part].reshape(SC // WIDTH, WIDTH, NEV).astype(BF16)


def project(half, src, group, eigvecs, solutions, blocks=2):
    depth = eigvecs.shape[2] // blocks

    def place(i, kb, src_ref, group_ref):
        slots = slot_timeslices(lambda s: src_ref[s], group_ref[0])
        return (0, timeslice_at(slots, half * HALF + i), kb, 0)

    spec = pl.BlockSpec((2, 1, depth, NEV), place)
    return pl.pallas_call(
        project_kernel,
        grid_spec=pltpu.PrefetchScalarGridSpec(
            num_scalar_prefetch=2,
            grid=(HALF, blocks),
            in_specs=[spec, spec],
            out_specs=pl.BlockSpec((SC // WIDTH, 1, 2, WIDTH, NEV), lambda i, kb, *_: (0, i, 0, 0, 0)),
            scratch_shapes=[pltpu.VMEM((2, SC, NEV), F32)],
        ),
        out_shape=jax.ShapeDtypeStruct((SC // WIDTH, HALF, 2, WIDTH, NEV), BF16),
        compiler_params=pltpu.CompilerParams(vmem_limit_bytes=58 * 2**20),
        cost_estimate=pl.CostEstimate(flops=1_400_000_000, bytes_accessed=6_000_000, transcendentals=0),
        name="project%d" % half,
    )(src, group, eigvecs, solutions)


def gather_rows(src_ref, group, half, projected, scatter_ref):
    slots = slot_timeslices(lambda s: src_ref[s], group)
    for s in range(NS):
        place = slot_of(slots, lax.rem(src_ref[s], TD)) - half * HALF
        place = jnp.clip(place, 0, HALF - 1)
        for part in range(2):
            rows = projected[0, part]
            for k in range(1, HALF):
                rows = jnp.where(place == k, projected[k, part], rows)
            for side in range(2):
                scatter_ref[(s * 2 + part) * 2 + side] = rows[:, side * 128 : (side + 1) * 128]


def weigh(src_ref, group, half, projected, elem_ref, weighted):
    slots = slot_timeslices(lambda s: src_ref[s], group)
    for k in range(HALF):
        t = timeslice_at(slots, half * HALF + k)
        er = elem_ref[0, t]
        ei = elem_ref[1, t]
        both = projected[k].reshape(2 * WIDTH, NEV)
        by_real = jnp.dot(both, er, preferred_element_type=F32)
        by_imag = jnp.dot(both, ei, preferred_element_type=F32)
        weighted(k, 0, (by_real[:WIDTH] + by_imag[WIDTH:]).astype(BF16))
        weighted(k, 1, (by_real[WIDTH:] - by_imag[:WIDTH]).astype(BF16))


def reduced(recv_ref):
    total = recv_ref[0].astype(F32)
    for c in range(1, recv_ref.shape[0]):
        total = total + recv_ref[c].astype(F32)
    return total.astype(BF16)


def first_kernel(src_ref, group_ref, recv_ref, elem_ref, scatter_ref, weighted_ref):
    group = group_ref[0]
    projected = reduced(recv_ref)
    gather_rows(src_ref, group, 0, projected, scatter_ref)

    def store(k, part, value):
        weighted_ref[k, part] = value

    weigh(src_ref, group, 0, projected, elem_ref, store)


def second_kernel(src_ref, group_ref, owner_ref, recv_ref, elem_ref, before_ref, scatter_ref, out_ref, all_ref):
    group = group_ref[0]
    projected = reduced(recv_ref)
    gather_rows(src_ref, group, 1, projected, scatter_ref)
    for k in range(HALF):
        all_ref[k] = before_ref[k]

    def store(k, part, value):
        all_ref[HALF + k, part] = value

    weigh(src_ref, group, 1, projected, elem_ref, store)
    slots = slot_timeslices(lambda s: src_ref[s], group)
    for j in range(TD * NS):
        out_ref[owner_ref[group, j]] = all_ref[slots[j // NS]]


def final_kernel(owner_ref, order_ref, where_ref, weighted_ref, own_ref, other_ref, out_ref):
    me = where_ref[0]
    side = where_ref[1]
    order = order_ref[...]
    wide = jnp.concatenate([order + spin * (SC // SPINS) for spin in range(SPINS)], axis=1)
    rows = lax.broadcasted_iota(jnp.int32, (SC, SC), 0)
    chosen = (rows == wide).astype(BF16)
    scale = (2.0 * NEV) ** (-0.5)
    dims = (((1,), (1,)), ((), ()))
    for e in range(out_ref.shape[0]):
        source = jnp.int32(0)
        for j in range(TD * NS):
            source = jnp.where(owner_ref[e, j] == me, j % NS, source)
        both = weighted_ref[e].reshape(2 * WIDTH, NEV)
        low, high = both[:, :128], both[:, 128:]
        mine = jnp.where(side == 0, low, high)
        rest = jnp.where(side == 0, high, low)
        by = []
        for part in range(2):
            value = lax.dot_general(mine, own_ref[source * 2 + part], dims, preferred_element_type=F32)
            value += lax.dot_general(rest, other_ref[source * 2 + part], dims, preferred_element_type=F32)
            by.append(value)
        real = (by[0][:WIDTH] + by[1][WIDTH:]) * scale
        imag = (by[1][:WIDTH] - by[0][WIDTH:]) * scale
        tile = jnp.concatenate([real, imag], axis=0).astype(BF16)
        tile = jnp.dot(tile, chosen, preferred_element_type=F32).astype(BF16)
        out_ref[e] = tile.reshape(2, WIDTH, SC)


def vmem():
    return pl.BlockSpec(memory_space=pltpu.VMEM)


def all_to_all(x, axes):
    return lax.all_to_all(x, axes, split_axis=0, concat_axis=0, tiled=True)


def spread(scatter, src):
    parts = all_to_all(scatter, TM)
    root = src[lax.axis_index(TM) // 4] // TD
    piece = lax.dynamic_index_in_dim(parts, root, 0, keepdims=True)
    slabs = all_to_all(jnp.broadcast_to(piece, parts.shape), SPACE)
    slabs = slabs.reshape(1, SC, 128)
    own = all_to_all(jnp.broadcast_to(slabs, (8, SC, 128)), ("yl", "x"))
    other = lax.ppermute(own, "core", [(0, 1), (1, 0)])
    return own, other


def per_device(eigvecs, solutions, elementals, source_list, pair_owner, dilution_order):
    me = lax.axis_index(TM)
    group = me.reshape(1)
    params = pltpu.CompilerParams(vmem_limit_bytes=40 * 2**20)
    sums = []
    for half in range(2):
        sums.append(project(half, source_list, group, eigvecs, solutions))
    recv = all_to_all(sums[0], SPACE)
    scatter, weighted = pl.pallas_call(
        first_kernel,
        in_specs=[smem(), smem(), vmem(), vmem()],
        out_specs=[vmem(), vmem()],
        out_shape=[
            jax.ShapeDtypeStruct((16, WIDTH, 128), BF16),
            jax.ShapeDtypeStruct((HALF, 2, WIDTH, NEV), BF16),
        ],
        compiler_params=params,
        name="first",
    )(source_list, group, recv, elementals)
    own, other = spread(scatter, source_list)
    recv = all_to_all(sums[1], SPACE)
    late, outgoing = pl.pallas_call(
        second_kernel,
        in_specs=[smem(), smem(), smem(), vmem(), vmem(), vmem()],
        out_specs=[vmem(), vmem()],
        out_shape=[
            jax.ShapeDtypeStruct((16, WIDTH, 128), BF16),
            jax.ShapeDtypeStruct((16, 2, WIDTH, NEV), BF16),
        ],
        scratch_shapes=[pltpu.VMEM((TD, 2, WIDTH, NEV), BF16)],
        compiler_params=params,
        name="second",
    )(source_list, group, pair_owner, recv, elementals, weighted)
    weights = all_to_all(outgoing, TM)

    first = source_list
    groups = first // TD
    distinct = jnp.array(True)
    same = (first[:, None] == first[None, :]) & (jnp.arange(NS)[:, None] > jnp.arange(NS)[None, :])
    fresh = ~jnp.any(same, axis=1)
    lower = (groups[:, None] == groups[None, :]) & (first[None, :] < first[:, None]) & fresh[None, :]
    rank = jnp.sum(lower.astype(jnp.int32), axis=1)
    is_late = rank >= HALF
    del distinct

    def again(own, other, late):
        own2, other2 = spread(late, source_list)
        pick = jnp.repeat(is_late, 2)[:, None, None]
        return jnp.where(pick, own2, own), jnp.where(pick, other2, other)

    own, other = lax.cond(jnp.any(is_late), again, lambda own, other, late: (own, other), own, other, late)

    where = jnp.stack([me, lax.axis_index("core")])
    return pl.pallas_call(
        final_kernel,
        in_specs=[smem(), vmem(), smem(), vmem(), vmem(), vmem()],
        out_specs=vmem(),
        out_shape=jax.ShapeDtypeStruct((16, 2, WIDTH, SC), BF16),
        compiler_params=params,
        name="final",
    )(pair_owner, dilution_order.reshape(1, -1), where, weights, own, other)


def solution(mesh):
    fine = Mesh(mesh.devices.reshape(2, 4, 2, 2, 8), TM + SPACE)
    in_specs = (
        P(None, TM, SPACE, None),
        P(None, TM, SPACE, None),
        P(None, TM, None, None),
        P(),
        P(),
        P(),
    )
    return jax.shard_map(
        per_device, mesh=fine, in_specs=in_specs, out_specs=P(TM, None, SPACE, None), check_vma=False
    )
```

```python
import functools

import jax
import jax.numpy as jnp
from jax import lax
from jax.experimental import pallas as pl
from jax.experimental.pallas import tpu as pltpu
from jax.sharding import Mesh
from jax.sharding import PartitionSpec as P

TM = ("yl", "x", "core")
SPACE = ("yh", "z")
TD = 4
NS = 4
NC = 16
NEV = 256
SC = 256
WIDTH = 16
SPINS = 4
LANES = 128
F32 = jnp.float32
BF16 = jnp.bfloat16
PARAMS = pltpu.CompilerParams(vmem_limit_bytes=40 * 2**20)


def smem():
    return pl.BlockSpec(memory_space=pltpu.SMEM)


def vmem():
    return pl.BlockSpec(memory_space=pltpu.VMEM)


def project_kernel(vec_hbm, sol_hbm, out_ref, vec_ref, sol_ref, sems):
    copies = []
    for t in range(TD):
        for part in range(2):
            copies.append(pltpu.make_async_copy(vec_hbm.at[part, t], vec_ref.at[t, part], sems.at[t, part, 0]))
            copies.append(pltpu.make_async_copy(sol_hbm.at[part, t], sol_ref.at[t, part], sems.at[t, part, 1]))
    for copy in copies:
        copy.start()
    dims = (((0,), (0,)), ((), ()))
    for t in range(TD):
        for copy in copies[4 * t : 4 * t + 4]:
            copy.wait()
        depth = vec_ref.shape[2]
        sol = sol_ref[t].reshape(2 * depth, SC)
        straight = vec_ref[t].reshape(2 * depth, NEV)
        turned = jnp.concatenate([-vec_ref[t, 1], vec_ref[t, 0]], axis=0)
        for part, right in enumerate((straight, turned)):
            value = lax.dot_general(sol, right, dims, preferred_element_type=F32).astype(BF16)
            out_ref[:, t, part] = value.reshape(NC, WIDTH, NEV)


def project(eigvecs, solutions):
    depth = eigvecs.shape[2]
    return pl.pallas_call(
        project_kernel,
        in_specs=[pl.BlockSpec(memory_space=pl.ANY)] * 2,
        out_specs=vmem(),
        out_shape=jax.ShapeDtypeStruct((NC, TD, 2, WIDTH, NEV), BF16),
        scratch_shapes=[
            pltpu.VMEM((TD, 2, depth, NEV), BF16),
            pltpu.VMEM((TD, 2, depth, SC), BF16),
            pltpu.SemaphoreType.DMA((TD, 2, 2)),
        ],
        compiler_params=pltpu.CompilerParams(vmem_limit_bytes=58 * 2**20),
        cost_estimate=pl.CostEstimate(flops=2_800_000_000, bytes_accessed=12_000_000, transcendentals=0),
        name="project",
    )(eigvecs, solutions)


def masks_kernel(src_ref, owner_ref, place_ref, root_ref, source_ref):
    me = lax.axis_index(TM)
    full = functools.partial(jnp.full, (8, LANES), dtype=jnp.int32)
    for s in range(NS):
        for t in range(TD):
            place_ref[s * TD + t] = full((lax.rem(src_ref[s], TD) == t).astype(jnp.int32))
    mine = lax.div(src_ref[lax.div(me, 4)], TD)
    for e in range(NC):
        root_ref[e] = full((mine == e).astype(jnp.int32))
        source = jnp.int32(0)
        for j in range(TD * NS):
            source = jnp.where(owner_ref[e, j] == me, j % NS, source)
        source_ref[e] = full(source)


def reduce_kernel(place_ref, recv_ref, total_ref, scatter_ref):
    totals = []
    for t in range(TD):
        total = recv_ref[0, t].astype(F32)
        for c in range(1, NC):
            total = total + recv_ref[c, t].astype(F32)
        total_ref[t] = total.astype(BF16)
        totals.append(total)
    for s in range(NS):
        for part in range(2):
            for side in range(2):
                lanes = slice(side * LANES, (side + 1) * LANES)
                rows = totals[0][part, :, lanes]
                for t in range(1, TD):
                    mask = place_ref[s * TD + t]
                    rows = jnp.where(jnp.concatenate([mask, mask]) != 0, totals[t][part, :, lanes], rows)
                scatter_ref[(s * 2 + part) * 2 + side] = rows.astype(BF16)


def weigh_kernel(owner_ref, total_ref, elem_ref, out_ref, all_ref):
    for t in range(TD):
        both = total_ref[t].reshape(2 * WIDTH, NEV)
        by_real = jnp.dot(both, elem_ref[0, t], preferred_element_type=F32)
        by_imag = jnp.dot(both, elem_ref[1, t], preferred_element_type=F32)
        all_ref[t, :WIDTH] = (by_real[:WIDTH] + by_imag[WIDTH:]).astype(BF16)
        all_ref[t, WIDTH:] = (by_real[WIDTH:] - by_imag[:WIDTH]).astype(BF16)
    group = lax.axis_index(TM)
    for j in range(TD * NS):
        out_ref[owner_ref[group, j]] = all_ref[j // NS]


def pick_kernel(root_ref, parts_ref, out_ref):
    part = parts_ref[0].astype(F32)
    for e in range(1, NC):
        mask = root_ref[e]
        part = jnp.where(jnp.concatenate([mask, mask]) != 0, parts_ref[e].astype(F32), part)
    part = part.astype(BF16)
    for c in range(NC):
        out_ref[c] = part


def pack_kernel(order_ref, rows_ref, weighted_ref, out_ref):
    order = order_ref[...]
    wide = jnp.concatenate([order + spin * (SC // SPINS) for spin in range(SPINS)], axis=1)
    chosen = (lax.broadcasted_iota(jnp.int32, (SC, SC), 0) == wide).astype(BF16)
    rows = rows_ref[...].reshape(SC, LANES)
    dims = (((0,), (0,)), ((), ()))
    part = lax.dot_general(rows, chosen, dims, preferred_element_type=F32).astype(BF16)
    part = part.reshape(4, 2 * WIDTH, SC)
    for pair in range(8):
        out_ref[pair, :4] = part
        out_ref[pair, 4:] = weighted_ref[2 * pair : 2 * pair + 2]


def final_kernel(source_ref, own_ref, other_ref, out_ref, sources_ref, left_ref, sum_ref):
    side = lax.axis_index("core")
    refs = ((own_ref, side), (other_ref, 1 - side))
    for k in range(2 * NS):
        for ref, at in refs:
            rows = pl.ds(pl.multiple_of(at * LANES, LANES), LANES)
            sources_ref[k, rows] = ref[k, :4].reshape(LANES, SC)
    block = 2 * WIDTH
    for pair in range(8):
        for which, (ref, at) in enumerate(refs):
            left_ref[which * 8 + pair] = ref[pair, 4 + side]
    left = left_ref[...].reshape(NC * block, NEV)
    for s in range(NS):
        for part in range(2):
            value = jnp.dot(left, sources_ref[s * 2 + part], preferred_element_type=F32)
            value = value.reshape(NC, block, SC)
            if s == 0:
                sum_ref[part] = value
                continue
            for which, (ref, at) in enumerate(refs):
                for pair in range(8):
                    row = which * 8 + pair
                    mask = source_ref[2 * pair + at] == s
                    mask = jnp.tile(mask, (block // 8, SC // LANES))
                    sum_ref[part, row] = jnp.where(mask, value[row], sum_ref[part, row])
    scale = (2.0 * NEV) ** (-0.5)
    for pair in range(8):
        for which, (ref, at) in enumerate(refs):
            e = 2 * pair + at
            by_real = sum_ref[0, which * 8 + pair]
            by_imag = sum_ref[1, which * 8 + pair]
            out_ref[e, 0] = ((by_real[:WIDTH] + by_imag[WIDTH:]) * scale).astype(BF16)
            out_ref[e, 1] = ((by_imag[:WIDTH] - by_real[WIDTH:]) * scale).astype(BF16)


def all_to_all(x, axes):
    return lax.all_to_all(x, axes, split_axis=0, concat_axis=0, tiled=True)


def per_device(eigvecs, solutions, elementals, source_list, pair_owner, dilution_order):
    mask = jax.ShapeDtypeStruct((NC, 8, LANES), jnp.int32)
    place, root, source = pl.pallas_call(
        masks_kernel,
        in_specs=[smem(), smem()],
        out_specs=[vmem()] * 3,
        out_shape=[mask] * 3,
        compiler_params=PARAMS,
        name="masks",
    )(source_list, pair_owner)

    recv = all_to_all(project(eigvecs, solutions), SPACE)
    total, scatter = pl.pallas_call(
        reduce_kernel,
        in_specs=[vmem()] * 2,
        out_specs=[vmem()] * 2,
        out_shape=[
            jax.ShapeDtypeStruct((TD, 2, WIDTH, NEV), BF16),
            jax.ShapeDtypeStruct((NC, WIDTH, LANES), BF16),
        ],
        compiler_params=PARAMS,
        name="reduce",
    )(place, recv)

    picked = pl.pallas_call(
        pick_kernel,
        in_specs=[vmem()] * 2,
        out_specs=vmem(),
        out_shape=jax.ShapeDtypeStruct((NC, WIDTH, LANES), BF16),
        compiler_params=PARAMS,
        name="pick",
    )(root, all_to_all(scatter, TM))
    rows = all_to_all(picked, SPACE)

    weighted = pl.pallas_call(
        weigh_kernel,
        in_specs=[smem(), vmem(), vmem()],
        out_specs=vmem(),
        out_shape=jax.ShapeDtypeStruct((NC, 2 * WIDTH, NEV), BF16),
        scratch_shapes=[pltpu.VMEM((TD, 2 * WIDTH, NEV), BF16)],
        compiler_params=PARAMS,
        cost_estimate=pl.CostEstimate(flops=70_000_000, bytes_accessed=2_000_000, transcendentals=0),
        name="weigh",
    )(pair_owner, total, elementals)

    packed = pl.pallas_call(
        pack_kernel,
        in_specs=[vmem()] * 3,
        out_specs=vmem(),
        out_shape=jax.ShapeDtypeStruct((8, 6, 2 * WIDTH, NEV), BF16),
        compiler_params=PARAMS,
        name="pack",
    )(dilution_order.reshape(1, -1), rows, weighted)
    own = all_to_all(packed, ("yl", "x"))
    other = lax.ppermute(own, "core", [(0, 1), (1, 0)])

    return pl.pallas_call(
        final_kernel,
        in_specs=[vmem()] * 3,
        out_specs=vmem(),
        out_shape=jax.ShapeDtypeStruct((NC, 2, WIDTH, SC), BF16),
        scratch_shapes=[
            pltpu.VMEM((2 * NS, NEV, SC), BF16),
            pltpu.VMEM((NC, 2 * WIDTH, NEV), BF16),
            pltpu.VMEM((2, NC, 2 * WIDTH, SC), F32),
        ],
        compiler_params=PARAMS,
        name="final",
    )(source, own, other)


def solution(mesh):
    fine = Mesh(mesh.devices.reshape(2, 4, 2, 2, 8), TM + SPACE)
    in_specs = (
        P(None, TM, SPACE, None),
        P(None, TM, SPACE, None),
        P(None, TM, None, None),
        P(),
        P(),
        P(),
    )
    return jax.shard_map(
        per_device, mesh=fine, in_specs=in_specs, out_specs=P(TM, None, SPACE, None), check_vma=False
    )
```

```python
import functools

import jax
import jax.numpy as jnp
from jax import lax
from jax.experimental import pallas as pl
from jax.experimental.pallas import tpu as pltpu
from jax.sharding import Mesh
from jax.sharding import PartitionSpec as P

TM = ("yl", "x", "core")
SPACE = ("yh", "z")
TD = 4
HALF = 2
NZ = 8
NS = 4
NC = 16
NEV = 256
SC = 256
WIDTH = 16
SPINS = 4
LANES = 128
F32 = jnp.float32
BF16 = jnp.bfloat16
PARAMS = pltpu.CompilerParams(vmem_limit_bytes=40 * 2**20)


def smem():
    return pl.BlockSpec(memory_space=pltpu.SMEM)


def vmem():
    return pl.BlockSpec(memory_space=pltpu.VMEM)


def slot_list(src, group):
    flags = []
    for t in range(TD):
        hit = src(0) == group * TD + t
        for s in range(1, NS):
            hit = jnp.logical_or(hit, src(s) == group * TD + t)
        flags.append(hit.astype(jnp.int32))
    total = flags[0] + flags[1] + flags[2] + flags[3]
    slots = []
    before = jnp.int32(0)
    for t in range(TD):
        slots.append(jnp.where(flags[t] == 1, before, total + t - before))
        before = before + flags[t]
    return slots


def slot_of(slots, t):
    out = slots[0]
    for k in range(1, TD):
        out = jnp.where(t == k, slots[k], out)
    return out


def timeslice_at(slots, place):
    out = jnp.int32(0)
    for t in range(1, TD):
        out = jnp.where(slots[t] == place, t, out)
    return out


def my_slots(src_ref):
    return slot_list(lambda s: src_ref[s], lax.axis_index(TM))


def project_kernel(half, src_ref, vec_hbm, sol_hbm, *refs):
    outs, (vec_ref, sol_ref, sems) = refs[: 1 + half * 7], refs[1 + half * 7 : 4 + half * 7]
    slots = my_slots(src_ref)
    copies = []
    for k in range(HALF):
        t = timeslice_at(slots, half * HALF + k)
        for part in range(2):
            copies.append(pltpu.make_async_copy(vec_hbm.at[part, t], vec_ref.at[k, part], sems.at[k, part, 0]))
            copies.append(pltpu.make_async_copy(sol_hbm.at[part, t], sol_ref.at[k, part], sems.at[k, part, 1]))
    for copy in copies:
        copy.start()
    dims = (((0,), (0,)), ((), ()))
    for k in range(HALF):
        for copy in copies[4 * k : 4 * k + 4]:
            copy.wait()
        depth = vec_ref.shape[2]
        sol = sol_ref[k].reshape(2 * depth, SC)
        straight = vec_ref[k].reshape(2 * depth, NEV)
        turned = jnp.concatenate([-vec_ref[k, 1], vec_ref[k, 0]], axis=0)
        for part, right in enumerate((straight, turned)):
            value = lax.dot_general(sol, right, dims, preferred_element_type=F32).astype(BF16)
            if half == 0:
                outs[0][:, k, part] = value.reshape(NC, WIDTH, NEV)
            else:
                value = value.reshape(2, NZ, WIDTH, NEV)
                for yh in range(2):
                    refs[-1][:, yh, k, part] = value[yh]
    if half == 1:
        z = lax.axis_index("z")
        for d in range(NZ):
            outs[d][...] = refs[-1][lax.rem(z + d, NZ)]


def project(half, src, eigvecs, solutions):
    depth = eigvecs.shape[2]
    scratch = [
        pltpu.VMEM((HALF, 2, depth, NEV), BF16),
        pltpu.VMEM((HALF, 2, depth, SC), BF16),
        pltpu.SemaphoreType.DMA((HALF, 2, 2)),
    ]
    if half == 0:
        shapes = [jax.ShapeDtypeStruct((NC, HALF, 2, WIDTH, NEV), BF16)]
    else:
        shapes = [jax.ShapeDtypeStruct((2, HALF, 2, WIDTH, NEV), BF16)] * NZ
        scratch.append(pltpu.VMEM((NZ, 2, HALF, 2, WIDTH, NEV), BF16))
    return pl.pallas_call(
        functools.partial(project_kernel, half),
        in_specs=[smem()] + [pl.BlockSpec(memory_space=pl.ANY)] * 2,
        out_specs=[vmem()] * len(shapes),
        out_shape=shapes,
        scratch_shapes=scratch,
        compiler_params=pltpu.CompilerParams(vmem_limit_bytes=(58, 50)[half] * 2**20),
        cost_estimate=pl.CostEstimate(flops=1_400_000_000, bytes_accessed=6_000_000, transcendentals=0),
        name="project%d" % half,
    )(src, eigvecs, solutions)


def masks_kernel(src_ref, owner_ref, place_ref, root_ref, source_ref):
    me = lax.axis_index(TM)
    slots = my_slots(src_ref)
    full = functools.partial(jnp.full, (8, LANES), dtype=jnp.int32)
    for s in range(NS):
        place = slot_of(slots, lax.rem(src_ref[s], TD))
        for k in range(TD):
            place_ref[s * TD + k] = full((place == k).astype(jnp.int32))
    mine = lax.div(src_ref[lax.div(me, 4)], TD)
    for e in range(NC):
        root_ref[e] = full((mine == e).astype(jnp.int32))
        source = jnp.int32(0)
        for j in range(TD * NS):
            source = jnp.where(owner_ref[e, j] == me, j % NS, source)
        source_ref[e] = full(source)


def scatter_sources(place_ref, half, totals, scatter_ref):
    for s in range(NS):
        for part in range(2):
            for side in range(2):
                lanes = slice(side * LANES, (side + 1) * LANES)
                rows = totals[0][part, :, lanes]
                for k in range(1, HALF):
                    mask = place_ref[s * TD + half * HALF + k]
                    rows = jnp.where(jnp.concatenate([mask, mask]) != 0, totals[k][part, :, lanes], rows)
                scatter_ref[(s * 2 + part) * 2 + side] = rows.astype(BF16)


def reduce_kernel(place_ref, recv_ref, total_ref, scatter_ref):
    totals = []
    for k in range(HALF):
        total = recv_ref[0, k].astype(F32)
        for c in range(1, NC):
            total = total + recv_ref[c, k].astype(F32)
        total_ref[k] = total.astype(BF16)
        totals.append(total)
    scatter_sources(place_ref, 0, totals, scatter_ref)


def sum_kernel(after_ref, *refs):
    del after_ref
    terms, (keep_ref, send_ref) = refs[:NZ], refs[NZ:]
    yh = lax.axis_index("yh")
    for ref, at in ((keep_ref, yh), (send_ref, 1 - yh)):
        total = terms[0][at].astype(F32)
        for term in terms[1:]:
            total = total + term[at].astype(F32)
        ref[...] = total


def second_sum(terms, after):
    keep, send = pl.pallas_call(
        sum_kernel,
        in_specs=[pl.BlockSpec(memory_space=pl.ANY)] + [vmem()] * NZ,
        out_specs=[vmem()] * 2,
        out_shape=[jax.ShapeDtypeStruct((HALF, 2, WIDTH, NEV), F32)] * 2,
        compiler_params=PARAMS,
        cost_estimate=pl.CostEstimate(flops=500_000, bytes_accessed=500_000, transcendentals=0),
        name="second_sum",
    )(after, *terms)
    return keep, lax.ppermute(send, "yh", [(0, 1), (1, 0)])


def weigh_kernel(src_ref, owner_ref, place_ref, early_ref, keep_ref, recv_ref, elem_ref, out_ref, late_ref, all_ref):
    slots = my_slots(src_ref)
    totals = [keep_ref[k] + recv_ref[k] for k in range(HALF)]
    scatter_sources(place_ref, 1, totals, late_ref)
    for k in range(TD):
        t = timeslice_at(slots, k)
        both = early_ref[k] if k < HALF else totals[k - HALF].astype(BF16)
        both = both.reshape(2 * WIDTH, NEV)
        by_real = jnp.dot(both, elem_ref[0, t], preferred_element_type=F32)
        by_imag = jnp.dot(both, elem_ref[1, t], preferred_element_type=F32)
        all_ref[k, :WIDTH] = (by_real[:WIDTH] + by_imag[WIDTH:]).astype(BF16)
        all_ref[k, WIDTH:] = (by_real[WIDTH:] - by_imag[:WIDTH]).astype(BF16)
    group = lax.axis_index(TM)
    for j in range(TD * NS):
        out_ref[owner_ref[group, j]] = all_ref[slots[j // NS]]


def pick_kernel(root_ref, parts_ref, out_ref):
    part = parts_ref[0].astype(F32)
    for e in range(1, NC):
        mask = root_ref[e]
        part = jnp.where(jnp.concatenate([mask, mask]) != 0, parts_ref[e].astype(F32), part)
    part = part.astype(BF16)
    for c in range(NC):
        out_ref[c] = part


def pack_kernel(order_ref, rows_ref, *refs):
    out_ref = refs[-1]
    order = order_ref[...]
    wide = jnp.concatenate([order + spin * (SC // SPINS) for spin in range(SPINS)], axis=1)
    chosen = (lax.broadcasted_iota(jnp.int32, (SC, SC), 0) == wide).astype(BF16)
    rows = rows_ref[...].reshape(SC, LANES)
    dims = (((0,), (0,)), ((), ()))
    part = lax.dot_general(rows, chosen, dims, preferred_element_type=F32).astype(BF16)
    part = part.reshape(4, 2 * WIDTH, SC)
    for pair in range(8):
        out_ref[pair, :4] = part
        if len(refs) > 1:
            out_ref[pair, 4:] = refs[0][2 * pair : 2 * pair + 2]


def final_kernel(source_ref, own_ref, other_ref, out_ref, sources_ref, left_ref, sum_ref):
    side = lax.axis_index("core")
    refs = ((own_ref, side), (other_ref, 1 - side))
    for k in range(2 * NS):
        for ref, at in refs:
            rows = pl.ds(pl.multiple_of(at * LANES, LANES), LANES)
            sources_ref[k, rows] = ref[k, :4].reshape(LANES, SC)
    block = 2 * WIDTH
    for pair in range(8):
        for which, (ref, at) in enumerate(refs):
            left_ref[which * 8 + pair] = ref[pair, 4 + side]
    left = left_ref[...].reshape(NC * block, NEV)
    for s in range(NS):
        for part in range(2):
            value = jnp.dot(left, sources_ref[s * 2 + part], preferred_element_type=F32)
            value = value.reshape(NC, block, SC)
            if s == 0:
                sum_ref[part] = value
                continue
            for which, (ref, at) in enumerate(refs):
                for pair in range(8):
                    row = which * 8 + pair
                    mask = source_ref[2 * pair + at] == s
                    mask = jnp.tile(mask, (block // 8, SC // LANES))
                    sum_ref[part, row] = jnp.where(mask, value[row], sum_ref[part, row])
    scale = (2.0 * NEV) ** (-0.5)
    for pair in range(8):
        for which, (ref, at) in enumerate(refs):
            e = 2 * pair + at
            by_real = sum_ref[0, which * 8 + pair]
            by_imag = sum_ref[1, which * 8 + pair]
            out_ref[e, 0] = ((by_real[:WIDTH] + by_imag[WIDTH:]) * scale).astype(BF16)
            out_ref[e, 1] = ((by_imag[:WIDTH] - by_real[WIDTH:]) * scale).astype(BF16)


def all_to_all(x, axes):
    return lax.all_to_all(x, axes, split_axis=0, concat_axis=0, tiled=True)


def spread(scatter, root):
    return pl.pallas_call(
        pick_kernel,
        in_specs=[vmem()] * 2,
        out_specs=vmem(),
        out_shape=jax.ShapeDtypeStruct((NC, WIDTH, LANES), BF16),
        compiler_params=PARAMS,
        cost_estimate=pl.CostEstimate(flops=100_000, bytes_accessed=200_000, transcendentals=0),
        name="pick",
    )(root, all_to_all(scatter, TM))


def gather(rows, order, *weighted):
    packed = pl.pallas_call(
        pack_kernel,
        in_specs=[vmem()] * (2 + len(weighted)),
        out_specs=vmem(),
        out_shape=jax.ShapeDtypeStruct((8, 4 + 2 * len(weighted), 2 * WIDTH, NEV), BF16),
        compiler_params=PARAMS,
        name="pack",
    )(order, rows, *weighted)
    own = all_to_all(packed, ("yl", "x"))
    return own, lax.ppermute(own, "core", [(0, 1), (1, 0)])


def late_sources(src):
    same = src[:, None] == src[None, :]
    earlier = jnp.arange(NS)[:, None] > jnp.arange(NS)[None, :]
    fresh = ~jnp.any(same & earlier, axis=1)
    groups = src // TD
    lower = (groups[:, None] == groups[None, :]) & (src[None, :] < src[:, None]) & fresh[None, :]
    return jnp.sum(lower.astype(jnp.int32), axis=1) >= HALF


def per_device(eigvecs, solutions, elementals, source_list, pair_owner, dilution_order):
    order = dilution_order.reshape(1, -1)
    mask = jax.ShapeDtypeStruct((NC, 8, LANES), jnp.int32)
    place, root, source = pl.pallas_call(
        masks_kernel,
        in_specs=[smem(), smem()],
        out_specs=[vmem()] * 3,
        out_shape=[mask] * 3,
        compiler_params=PARAMS,
        cost_estimate=pl.CostEstimate(flops=100_000, bytes_accessed=200_000, transcendentals=0),
        name="masks",
    )(source_list, pair_owner)

    (first,) = project(0, source_list, eigvecs, solutions)
    first, later = lax.optimization_barrier((first, source_list))
    recv = all_to_all(first, SPACE)
    early, scatter = pl.pallas_call(
        reduce_kernel,
        in_specs=[vmem()] * 2,
        out_specs=[vmem()] * 2,
        out_shape=[
            jax.ShapeDtypeStruct((HALF, 2, WIDTH, NEV), BF16),
            jax.ShapeDtypeStruct((NC, WIDTH, LANES), BF16),
        ],
        compiler_params=PARAMS,
        cost_estimate=pl.CostEstimate(flops=500_000, bytes_accessed=500_000, transcendentals=0),
        name="reduce",
    )(place, recv)

    terms = list(project(1, later, eigvecs, solutions))
    for d in range(1, NZ):
        terms[d] = lax.ppermute(terms[d], "z", [(z, (z + d) % NZ) for z in range(NZ)])
    picked = spread(scatter, root)
    rows = all_to_all(picked, SPACE)
    keep, added = second_sum(terms, picked)
    weighted, late = pl.pallas_call(
        weigh_kernel,
        in_specs=[smem(), smem()] + [vmem()] * 5,
        out_specs=[vmem()] * 2,
        out_shape=[
            jax.ShapeDtypeStruct((NC, 2 * WIDTH, NEV), BF16),
            jax.ShapeDtypeStruct((NC, WIDTH, LANES), BF16),
        ],
        scratch_shapes=[pltpu.VMEM((TD, 2 * WIDTH, NEV), BF16)],
        compiler_params=PARAMS,
        cost_estimate=pl.CostEstimate(flops=70_000_000, bytes_accessed=2_000_000, transcendentals=0),
        name="weigh",
    )(source_list, pair_owner, place, early, keep, added, elementals)

    own, other = gather(rows, order, weighted)

    is_late = late_sources(source_list)

    def again(own, other, late):
        own_late, other_late = gather(all_to_all(spread(late, root), SPACE), order)
        pick = jnp.repeat(is_late, 2)[:, None, None, None]
        own = own.at[:, :4].set(jnp.where(pick, own_late, own[:, :4]))
        other = other.at[:, :4].set(jnp.where(pick, other_late, other[:, :4]))
        return own, other

    own, other = lax.cond(jnp.any(is_late), again, lambda own, other, late: (own, other), own, other, late)

    return pl.pallas_call(
        final_kernel,
        in_specs=[vmem()] * 3,
        out_specs=vmem(),
        out_shape=jax.ShapeDtypeStruct((NC, 2, WIDTH, SC), BF16),
        scratch_shapes=[
            pltpu.VMEM((2 * NS, NEV, SC), BF16),
            pltpu.VMEM((NC, 2 * WIDTH, NEV), BF16),
            pltpu.VMEM((2, NC, 2 * WIDTH, SC), F32),
        ],
        compiler_params=PARAMS,
        name="final",
    )(source, own, other)


def solution(mesh):
    fine = Mesh(mesh.devices.reshape(2, 4, 2, 2, 8), TM + SPACE)
    in_specs = (
        P(None, TM, SPACE, None),
        P(None, TM, SPACE, None),
        P(None, TM, None, None),
        P(),
        P(),
        P(),
    )
    return jax.shard_map(
        per_device, mesh=fine, in_specs=in_specs, out_specs=P(TM, None, SPACE, None), check_vma=False
    )
```

```python
import functools

import jax
import jax.numpy as jnp
from jax import lax
from jax.experimental import pallas as pl
from jax.experimental.pallas import tpu as pltpu
from jax.sharding import Mesh
from jax.sharding import PartitionSpec as P

TM = ("yl", "x", "core")
SPACE = ("yh", "z")
TD = 4
HALF = 2
NZ = 8
NS = 4
NC = 16
NEV = 256
SC = 256
WIDTH = 16
SPINS = 4
LANES = 128
BLOCK = (2, HALF, 2, WIDTH, 256)
F32 = jnp.float32
BF16 = jnp.bfloat16
PARAMS = pltpu.CompilerParams(vmem_limit_bytes=40 * 2**20)


def smem():
    return pl.BlockSpec(memory_space=pltpu.SMEM)


def vmem():
    return pl.BlockSpec(memory_space=pltpu.VMEM)


def slot_list(src, group):
    flags = []
    for t in range(TD):
        hit = src(0) == group * TD + t
        for s in range(1, NS):
            hit = jnp.logical_or(hit, src(s) == group * TD + t)
        flags.append(hit.astype(jnp.int32))
    total = flags[0] + flags[1] + flags[2] + flags[3]
    slots = []
    before = jnp.int32(0)
    for t in range(TD):
        slots.append(jnp.where(flags[t] == 1, before, total + t - before))
        before = before + flags[t]
    return slots


def slot_of(slots, t):
    out = slots[0]
    for k in range(1, TD):
        out = jnp.where(t == k, slots[k], out)
    return out


def timeslice_at(slots, place):
    out = jnp.int32(0)
    for t in range(1, TD):
        out = jnp.where(slots[t] == place, t, out)
    return out


def my_slots(src_ref):
    return slot_list(lambda s: src_ref[s], lax.axis_index(TM))


def write_masks(src_ref, owner_ref, place_ref, root_ref, source_ref):
    me = lax.axis_index(TM)
    slots = my_slots(src_ref)
    full = functools.partial(jnp.full, (8, LANES), dtype=jnp.int32)
    for s in range(NS):
        place = slot_of(slots, lax.rem(src_ref[s], TD))
        for k in range(TD):
            place_ref[s * TD + k] = full((place == k).astype(jnp.int32))
    mine = lax.div(src_ref[lax.div(me, 4)], TD)
    for e in range(NC):
        root_ref[e] = full((mine == e).astype(jnp.int32))
        source = jnp.int32(0)
        for j in range(TD * NS):
            source = jnp.where(owner_ref[e, j] == me, j % NS, source)
        source_ref[e] = full(source)


def project_kernel(half, src_ref, owner_ref, vec_hbm, sol_hbm, *refs):
    outs, (vec_ref, sol_ref, sems) = refs[: 1 + half * 4], refs[1 + half * 4 : 4 + half * 4]
    slots = my_slots(src_ref)
    copies = []
    for k in range(HALF):
        t = timeslice_at(slots, half * HALF + k)
        for part in range(2):
            copies.append(pltpu.make_async_copy(vec_hbm.at[part, t], vec_ref.at[k, part], sems.at[k, part, 0]))
            copies.append(pltpu.make_async_copy(sol_hbm.at[part, t], sol_ref.at[k, part], sems.at[k, part, 1]))
    for copy in copies:
        copy.start()
    if half == 1:
        write_masks(src_ref, owner_ref, *outs[2:])
    dims = (((0,), (0,)), ((), ()))
    for k in range(HALF):
        for copy in copies[4 * k : 4 * k + 4]:
            copy.wait()
        depth = vec_ref.shape[2]
        sol = sol_ref[k].reshape(2 * depth, SC)
        straight = vec_ref[k].reshape(2 * depth, NEV)
        turned = jnp.concatenate([-vec_ref[k, 1], vec_ref[k, 0]], axis=0)
        for part, right in enumerate((straight, turned)):
            value = lax.dot_general(sol, right, dims, preferred_element_type=F32)
            if half == 0:
                outs[0][:, k, part] = value.astype(BF16).reshape(NC, WIDTH, NEV)
            else:
                value = value.reshape(2, NZ, WIDTH, NEV)
                for yh in range(2):
                    refs[-1][:, yh, k, part] = value[yh]
    if half == 1:
        parity = lax.rem(lax.axis_index("z"), 2)
        for k in range(NZ // 2):
            outs[0][k] = refs[-1][2 * k + parity]
            outs[1][k] = refs[-1][2 * k + 1 - parity].astype(BF16)


def project(half, src, owner, eigvecs, solutions):
    depth = eigvecs.shape[2]
    scratch = [
        pltpu.VMEM((HALF, 2, depth, NEV), BF16),
        pltpu.VMEM((HALF, 2, depth, SC), BF16),
        pltpu.SemaphoreType.DMA((HALF, 2, 2)),
    ]
    if half == 0:
        shapes = [jax.ShapeDtypeStruct((NC, HALF, 2, WIDTH, NEV), BF16)]
    else:
        shapes = [jax.ShapeDtypeStruct((NZ // 2,) + BLOCK, dtype) for dtype in (F32, BF16)]
        shapes += [jax.ShapeDtypeStruct((NC, 8, LANES), jnp.int32)] * 3
        scratch.append(pltpu.VMEM((NZ,) + BLOCK, F32))
    return pl.pallas_call(
        functools.partial(project_kernel, half),
        in_specs=[smem()] * 2 + [pl.BlockSpec(memory_space=pl.ANY)] * 2,
        out_specs=[vmem()] * len(shapes),
        out_shape=shapes,
        scratch_shapes=scratch,
        compiler_params=pltpu.CompilerParams(vmem_limit_bytes=(58, 50)[half] * 2**20),
        cost_estimate=pl.CostEstimate(flops=1_400_000_000, bytes_accessed=6_000_000, transcendentals=0),
        name="project%d" % half,
    )(src, owner, eigvecs, solutions)


def scatter_sources(place_ref, half, totals, scatter_ref):
    for s in range(NS):
        for part in range(2):
            for side in range(2):
                lanes = slice(side * LANES, (side + 1) * LANES)
                rows = totals[0][part, :, lanes]
                for k in range(1, HALF):
                    mask = place_ref[s * TD + half * HALF + k]
                    rows = jnp.where(jnp.concatenate([mask, mask]) != 0, totals[k][part, :, lanes], rows)
                scatter_ref[(s * 2 + part) * 2 + side] = rows.astype(BF16)


def reduce_kernel(place_ref, recv_ref, total_ref, scatter_ref):
    totals = []
    for k in range(HALF):
        total = recv_ref[0, k].astype(F32)
        for c in range(1, NC):
            total = total + recv_ref[c, k].astype(F32)
        total_ref[k] = total.astype(BF16)
        totals.append(total)
    scatter_sources(place_ref, 0, totals, scatter_ref)


def pair_kernel(after_ref, kept_ref, came_ref, own_ref, *send_refs):
    del after_ref
    half = lax.div(lax.axis_index("z"), 2)
    own_ref[...] = kept_ref[half] + came_ref[half].astype(F32)
    for d, ref in enumerate(send_refs):
        at = lax.rem(half + d + 1, NZ // 2)
        ref[...] = (kept_ref[at] + came_ref[at].astype(F32)).astype(BF16)


def sum_kernel(after_ref, own_ref, *refs):
    del after_ref
    terms, (keep_ref, send_ref) = refs[:-2], refs[-2:]
    yh = lax.axis_index("yh")
    for ref, at in ((keep_ref, yh), (send_ref, 1 - yh)):
        total = own_ref[at]
        for term in terms:
            total = total + term[at].astype(F32)
        ref[...] = total


def second_call(kernel, name, shapes, *operands):
    return pl.pallas_call(
        kernel,
        in_specs=[pl.BlockSpec(memory_space=pl.ANY)] + [vmem()] * (len(operands) - 1),
        out_specs=[vmem()] * len(shapes),
        out_shape=shapes,
        compiler_params=PARAMS,
        cost_estimate=pl.CostEstimate(flops=500_000, bytes_accessed=500_000, transcendentals=0),
        name=name,
    )(*operands)


def along_z(x, to):
    return lax.ppermute(x, "z", [(z, to(z)) for z in range(NZ)])


def weigh_kernel(src_ref, owner_ref, place_ref, early_ref, keep_ref, recv_ref, elem_ref, out_ref, late_ref, all_ref):
    slots = my_slots(src_ref)
    totals = [keep_ref[k] + recv_ref[k] for k in range(HALF)]
    scatter_sources(place_ref, 1, totals, late_ref)
    for k in range(TD):
        t = timeslice_at(slots, k)
        both = early_ref[k] if k < HALF else totals[k - HALF].astype(BF16)
        both = both.reshape(2 * WIDTH, NEV)
        by_real = jnp.dot(both, elem_ref[0, t], preferred_element_type=F32)
        by_imag = jnp.dot(both, elem_ref[1, t], preferred_element_type=F32)
        all_ref[k, :WIDTH] = (by_real[:WIDTH] + by_imag[WIDTH:]).astype(BF16)
        all_ref[k, WIDTH:] = (by_real[WIDTH:] - by_imag[:WIDTH]).astype(BF16)
    group = lax.axis_index(TM)
    for j in range(TD * NS):
        out_ref[owner_ref[group, j]] = all_ref[slots[j // NS]]


def pick_kernel(root_ref, parts_ref, out_ref):
    part = parts_ref[0].astype(F32)
    for e in range(1, NC):
        mask = root_ref[e]
        part = jnp.where(jnp.concatenate([mask, mask]) != 0, parts_ref[e].astype(F32), part)
    part = part.astype(BF16)
    for c in range(NC):
        out_ref[c] = part


def pack_kernel(order_ref, rows_ref, *refs):
    out_ref = refs[-1]
    order = order_ref[...]
    wide = jnp.concatenate([order + spin * (SC // SPINS) for spin in range(SPINS)], axis=1)
    chosen = (lax.broadcasted_iota(jnp.int32, (SC, SC), 0) == wide).astype(BF16)
    rows = rows_ref[...].reshape(SC, LANES)
    dims = (((0,), (0,)), ((), ()))
    part = lax.dot_general(rows, chosen, dims, preferred_element_type=F32).astype(BF16)
    part = part.reshape(4, 2 * WIDTH, SC)
    for pair in range(8):
        out_ref[pair, :4] = part
        if len(refs) > 1:
            out_ref[pair, 4:] = refs[0][2 * pair : 2 * pair + 2]


def final_kernel(source_ref, own_ref, other_ref, out_ref, sources_ref, left_ref, sum_ref):
    side = lax.axis_index("core")
    refs = ((own_ref, side), (other_ref, 1 - side))
    for k in range(2 * NS):
        for ref, at in refs:
            rows = pl.ds(pl.multiple_of(at * LANES, LANES), LANES)
            sources_ref[k, rows] = ref[k, :4].reshape(LANES, SC)
    block = 2 * WIDTH
    for pair in range(8):
        for which, (ref, at) in enumerate(refs):
            left_ref[which * 8 + pair] = ref[pair, 4 + side]
    left = left_ref[...].reshape(NC * block, NEV)
    for s in range(NS):
        for part in range(2):
            value = jnp.dot(left, sources_ref[s * 2 + part], preferred_element_type=F32)
            value = value.reshape(NC, block, SC)
            if s == 0:
                sum_ref[part] = value
                continue
            for which, (ref, at) in enumerate(refs):
                for pair in range(8):
                    row = which * 8 + pair
                    mask = source_ref[2 * pair + at] == s
                    mask = jnp.tile(mask, (block // 8, SC // LANES))
                    sum_ref[part, row] = jnp.where(mask, value[row], sum_ref[part, row])
    scale = (2.0 * NEV) ** (-0.5)
    for pair in range(8):
        for which, (ref, at) in enumerate(refs):
            e = 2 * pair + at
            by_real = sum_ref[0, which * 8 + pair]
            by_imag = sum_ref[1, which * 8 + pair]
            out_ref[e, 0] = ((by_real[:WIDTH] + by_imag[WIDTH:]) * scale).astype(BF16)
            out_ref[e, 1] = ((by_imag[:WIDTH] - by_real[WIDTH:]) * scale).astype(BF16)


def all_to_all(x, axes):
    return lax.all_to_all(x, axes, split_axis=0, concat_axis=0, tiled=True)


def spread(scatter, root):
    return pl.pallas_call(
        pick_kernel,
        in_specs=[vmem()] * 2,
        out_specs=vmem(),
        out_shape=jax.ShapeDtypeStruct((NC, WIDTH, LANES), BF16),
        compiler_params=PARAMS,
        cost_estimate=pl.CostEstimate(flops=100_000, bytes_accessed=200_000, transcendentals=0),
        name="pick",
    )(root, all_to_all(scatter, TM))


def gather(rows, order, *weighted):
    packed = pl.pallas_call(
        pack_kernel,
        in_specs=[vmem()] * (2 + len(weighted)),
        out_specs=vmem(),
        out_shape=jax.ShapeDtypeStruct((8, 4 + 2 * len(weighted), 2 * WIDTH, NEV), BF16),
        compiler_params=PARAMS,
        name="pack",
    )(order, rows, *weighted)
    own = all_to_all(packed, ("yl", "x"))
    return own, lax.ppermute(own, "core", [(0, 1), (1, 0)])


def late_sources(src):
    same = src[:, None] == src[None, :]
    earlier = jnp.arange(NS)[:, None] > jnp.arange(NS)[None, :]
    fresh = ~jnp.any(same & earlier, axis=1)
    groups = src // TD
    lower = (groups[:, None] == groups[None, :]) & (src[None, :] < src[:, None]) & fresh[None, :]
    return jnp.sum(lower.astype(jnp.int32), axis=1) >= HALF


def per_device(eigvecs, solutions, elementals, source_list, pair_owner, dilution_order):
    order = dilution_order.reshape(1, -1)
    (first,) = project(0, source_list, pair_owner, eigvecs, solutions)
    first, later = lax.optimization_barrier((first, source_list))
    recv = all_to_all(first, SPACE)
    kept, send, place, root, source = project(1, later, pair_owner, eigvecs, solutions)
    early, scatter = pl.pallas_call(
        reduce_kernel,
        in_specs=[vmem()] * 2,
        out_specs=[vmem()] * 2,
        out_shape=[
            jax.ShapeDtypeStruct((HALF, 2, WIDTH, NEV), BF16),
            jax.ShapeDtypeStruct((NC, WIDTH, LANES), BF16),
        ],
        compiler_params=PARAMS,
        cost_estimate=pl.CostEstimate(flops=500_000, bytes_accessed=500_000, transcendentals=0),
        name="reduce",
    )(place, recv)

    block = [jax.ShapeDtypeStruct(BLOCK, dtype) for dtype in (F32, BF16, BF16, BF16)]
    terms = list(second_call(pair_kernel, "pair", block, scatter, kept, along_z(send, lambda z: z ^ 1)))
    for d in range(1, NZ // 2):
        terms[d] = along_z(terms[d], lambda z: (z + 2 * d) % NZ)
    picked = spread(scatter, root)
    rows = all_to_all(picked, SPACE)
    keep, send = second_call(sum_kernel, "sum", [jax.ShapeDtypeStruct(BLOCK[1:], F32)] * 2, picked, *terms)
    added = lax.ppermute(send, "yh", [(0, 1), (1, 0)])
    weighted, late = pl.pallas_call(
        weigh_kernel,
        in_specs=[smem(), smem()] + [vmem()] * 5,
        out_specs=[vmem()] * 2,
        out_shape=[
            jax.ShapeDtypeStruct((NC, 2 * WIDTH, NEV), BF16),
            jax.ShapeDtypeStruct((NC, WIDTH, LANES), BF16),
        ],
        scratch_shapes=[pltpu.VMEM((TD, 2 * WIDTH, NEV), BF16)],
        compiler_params=PARAMS,
        cost_estimate=pl.CostEstimate(flops=70_000_000, bytes_accessed=2_000_000, transcendentals=0),
        name="weigh",
    )(source_list, pair_owner, place, early, keep, added, elementals)

    own, other = gather(rows, order, weighted)

    is_late = late_sources(source_list)

    def again(own, other, late):
        own_late, other_late = gather(all_to_all(spread(late, root), SPACE), order)
        pick = jnp.repeat(is_late, 2)[:, None, None, None]
        own = own.at[:, :4].set(jnp.where(pick, own_late, own[:, :4]))
        other = other.at[:, :4].set(jnp.where(pick, other_late, other[:, :4]))
        return own, other

    own, other = lax.cond(jnp.any(is_late), again, lambda own, other, late: (own, other), own, other, late)

    return pl.pallas_call(
        final_kernel,
        in_specs=[vmem()] * 3,
        out_specs=vmem(),
        out_shape=jax.ShapeDtypeStruct((NC, 2, WIDTH, SC), BF16),
        scratch_shapes=[
            pltpu.VMEM((2 * NS, NEV, SC), BF16),
            pltpu.VMEM((NC, 2 * WIDTH, NEV), BF16),
            pltpu.VMEM((2, NC, 2 * WIDTH, SC), F32),
        ],
        compiler_params=PARAMS,
        name="final",
    )(source, own, other)


def solution(mesh):
    fine = Mesh(mesh.devices.reshape(2, 4, 2, 2, 8), TM + SPACE)
    in_specs = (
        P(None, TM, SPACE, None),
        P(None, TM, SPACE, None),
        P(None, TM, None, None),
        P(),
        P(),
        P(),
    )
    return jax.shard_map(
        per_device, mesh=fine, in_specs=in_specs, out_specs=P(TM, None, SPACE, None), check_vma=False
    )
```

```python
import functools

import jax
import jax.numpy as jnp
from jax import lax
from jax.experimental import pallas as pl
from jax.experimental.pallas import tpu as pltpu
from jax.sharding import Mesh
from jax.sharding import PartitionSpec as P

TM = ("yl", "x", "core")
SPACE = ("yh", "z")
TD = 4
HALF = 2
NZ = 8
NS = 4
NC = 16
NEV = 256
SC = 256
WIDTH = 16
SPINS = 4
LANES = 128
BLOCK = (HALF, 2, WIDTH, 256)
F32 = jnp.float32
BF16 = jnp.bfloat16
PARAMS = pltpu.CompilerParams(vmem_limit_bytes=40 * 2**20)


def smem():
    return pl.BlockSpec(memory_space=pltpu.SMEM)


def vmem():
    return pl.BlockSpec(memory_space=pltpu.VMEM)


def slot_list(src, group):
    flags = []
    for t in range(TD):
        hit = src(0) == group * TD + t
        for s in range(1, NS):
            hit = jnp.logical_or(hit, src(s) == group * TD + t)
        flags.append(hit.astype(jnp.int32))
    total = flags[0] + flags[1] + flags[2] + flags[3]
    slots = []
    before = jnp.int32(0)
    for t in range(TD):
        slots.append(jnp.where(flags[t] == 1, before, total + t - before))
        before = before + flags[t]
    return slots


def slot_of(slots, t):
    out = slots[0]
    for k in range(1, TD):
        out = jnp.where(t == k, slots[k], out)
    return out


def timeslice_at(slots, place):
    out = jnp.int32(0)
    for t in range(1, TD):
        out = jnp.where(slots[t] == place, t, out)
    return out


def my_slots(src_ref):
    return slot_list(lambda s: src_ref[s], lax.axis_index(TM))


def write_masks(src_ref, owner_ref, place_ref, root_ref, source_ref, slot_ref):
    me = lax.axis_index(TM)
    slots = my_slots(src_ref)
    full = functools.partial(jnp.full, (8, LANES), dtype=jnp.int32)
    for s in range(NS):
        place = slot_of(slots, lax.rem(src_ref[s], TD))
        for k in range(TD):
            place_ref[s * TD + k] = full((place == k).astype(jnp.int32))
    mine = lax.div(src_ref[lax.div(me, 4)], TD)
    for e in range(NC):
        root_ref[e] = full((mine == e).astype(jnp.int32))
        source = jnp.int32(0)
        for j in range(TD * NS):
            source = jnp.where(owner_ref[e, j] == me, j % NS, source)
        source_ref[e] = full(source)
    for j in range(TD * NS):
        slot_ref[owner_ref[me, j]] = full(slots[j // NS])


def project_kernel(half, src_ref, vec_hbm, sol_hbm, *refs):
    if half == 1:
        (owner_ref, elem_ref), refs = refs[:2], refs[2:]
    outs, (vec_ref, sol_ref, sems) = refs[: 1 + half * 8], refs[1 + half * 8 : 4 + half * 8]
    slots = my_slots(src_ref)
    copies = []
    for k in range(HALF):
        t = timeslice_at(slots, half * HALF + k)
        for part in range(2):
            copies.append(pltpu.make_async_copy(vec_hbm.at[part, t], vec_ref.at[k, part], sems.at[k, part, 0]))
            copies.append(pltpu.make_async_copy(sol_hbm.at[part, t], sol_ref.at[k, part], sems.at[k, part, 1]))
    for copy in copies:
        copy.start()
    if half == 1:
        write_masks(src_ref, owner_ref, *outs[5:])
        for k in range(TD):
            for part in range(2):
                outs[4][k, part] = elem_ref[part, timeslice_at(slots, k)]
    dims = (((0,), (0,)), ((), ()))
    for k in range(HALF):
        for copy in copies[4 * k : 4 * k + 4]:
            copy.wait()
        depth = vec_ref.shape[2]
        sol = sol_ref[k].reshape(2 * depth, SC)
        straight = vec_ref[k].reshape(2 * depth, NEV)
        turned = jnp.concatenate([-vec_ref[k, 1], vec_ref[k, 0]], axis=0)
        for part, right in enumerate((straight, turned)):
            value = lax.dot_general(sol, right, dims, preferred_element_type=F32)
            if half == 0:
                outs[0][:, k, part] = value.astype(BF16).reshape(NC, WIDTH, NEV)
            else:
                value = value.reshape(2, NZ, WIDTH, NEV)
                for yh in range(2):
                    refs[-1][:, yh, k, part] = value[yh]
    if half == 1:
        parity = lax.rem(lax.axis_index("z"), 2)
        yh = lax.axis_index("yh")
        for k in range(NZ // 2):
            same, other = 2 * k + parity, 2 * k + 1 - parity
            outs[0][k] = refs[-1][same, yh]
            outs[1][k] = refs[-1][other, yh].astype(BF16)
            outs[2][k] = refs[-1][same, 1 - yh].astype(BF16)
            outs[3][k] = refs[-1][other, 1 - yh].astype(BF16)


def project(half, src, eigvecs, solutions, *more):
    depth = eigvecs.shape[2]
    scratch = [
        pltpu.VMEM((HALF, 2, depth, NEV), BF16),
        pltpu.VMEM((HALF, 2, depth, SC), BF16),
        pltpu.SemaphoreType.DMA((HALF, 2, 2)),
    ]
    if half == 0:
        shapes = [jax.ShapeDtypeStruct((NC, HALF, 2, WIDTH, NEV), BF16)]
    else:
        shapes = [jax.ShapeDtypeStruct((NZ // 2,) + BLOCK, dtype) for dtype in (F32, BF16, BF16, BF16)]
        shapes.append(jax.ShapeDtypeStruct((TD, 2, NEV, NEV), BF16))
        shapes += [jax.ShapeDtypeStruct((NC, 8, LANES), jnp.int32)] * 4
        scratch.append(pltpu.VMEM((NZ, 2) + BLOCK, F32))
    return pl.pallas_call(
        functools.partial(project_kernel, half),
        in_specs=[smem()] + [pl.BlockSpec(memory_space=pl.ANY)] * 2 + [smem(), vmem()][: len(more)],
        out_specs=[vmem()] * len(shapes),
        out_shape=shapes,
        scratch_shapes=scratch,
        compiler_params=pltpu.CompilerParams(vmem_limit_bytes=(58, 50)[half] * 2**20),
        cost_estimate=pl.CostEstimate(flops=1_400_000_000, bytes_accessed=6_000_000, transcendentals=0),
        name="project%d" % half,
    )(src, eigvecs, solutions, *more)


def scatter_sources(place_ref, half, totals, scatter_ref):
    for s in range(NS):
        for part in range(2):
            for side in range(2):
                lanes = slice(side * LANES, (side + 1) * LANES)
                rows = totals[0][part, :, lanes]
                for k in range(1, HALF):
                    mask = place_ref[s * TD + half * HALF + k]
                    rows = jnp.where(jnp.concatenate([mask, mask]) != 0, totals[k][part, :, lanes], rows)
                scatter_ref[(s * 2 + part) * 2 + side] = rows.astype(BF16)


def reduce_kernel(place_ref, recv_ref, total_ref, scatter_ref):
    totals = []
    for k in range(HALF):
        total = recv_ref[0, k].astype(F32)
        for c in range(1, NC):
            total = total + recv_ref[c, k].astype(F32)
        total_ref[k] = total.astype(BF16)
        totals.append(total)
    scatter_sources(place_ref, 0, totals, scatter_ref)


def pair_kernel(after_ref, kept_ref, *refs):
    del after_ref
    came_refs, own_ref, send_refs = refs[:3], refs[3], refs[4:]
    half = lax.div(lax.axis_index("z"), 2)
    for d in range(NZ // 2):
        at = lax.rem(half + d, NZ // 2)
        total = kept_ref[at]
        for ref in came_refs:
            total = total + ref[at].astype(F32)
        if d == 0:
            own_ref[...] = total
        else:
            send_refs[d - 1][...] = total.astype(BF16)


def along_z(x, to):
    return lax.ppermute(x, "z", [(z, to(z)) for z in range(NZ)])


def weigh_kernel(slot_ref, place_ref, early_ref, elem_ref, *refs):
    terms, (out_ref, late_ref) = refs[:-2], refs[-2:]
    totals = []
    for k in range(HALF):
        total = terms[0][k]
        for term in terms[1:]:
            total = total + term[k].astype(F32)
        totals.append(total)
    weighted = []
    for k in range(TD):
        both = early_ref[k] if k < HALF else totals[k - HALF].astype(BF16)
        both = both.reshape(2 * WIDTH, NEV)
        by_real = jnp.dot(both, elem_ref[k, 0], preferred_element_type=F32)
        by_imag = jnp.dot(both, elem_ref[k, 1], preferred_element_type=F32)
        real = by_real[:WIDTH] + by_imag[WIDTH:]
        imag = by_real[WIDTH:] - by_imag[:WIDTH]
        weighted.append(jnp.concatenate([real, imag], axis=0))
    for d in range(NC):
        slot = jnp.tile(slot_ref[d], (2 * WIDTH // 8, NEV // LANES))
        value = weighted[0]
        for k in range(1, TD):
            value = jnp.where(slot == k, weighted[k], value)
        out_ref[d] = value.astype(BF16)
    scatter_sources(place_ref, 1, totals, late_ref)


def pick_kernel(root_ref, parts_ref, out_ref):
    part = parts_ref[0].astype(F32)
    for e in range(1, NC):
        mask = root_ref[e]
        part = jnp.where(jnp.concatenate([mask, mask]) != 0, parts_ref[e].astype(F32), part)
    part = part.astype(BF16)
    for c in range(NC):
        out_ref[c] = part


def pack_kernel(order_ref, rows_ref, *refs):
    out_ref = refs[-1]
    order = order_ref[...]
    wide = jnp.concatenate([order + spin * (SC // SPINS) for spin in range(SPINS)], axis=1)
    chosen = (lax.broadcasted_iota(jnp.int32, (SC, SC), 0) == wide).astype(BF16)
    rows = rows_ref[...].reshape(SC, LANES)
    dims = (((0,), (0,)), ((), ()))
    part = lax.dot_general(rows, chosen, dims, preferred_element_type=F32).astype(BF16)
    part = part.reshape(4, 2 * WIDTH, SC)
    for pair in range(8):
        out_ref[pair, :4] = part
        if len(refs) > 1:
            out_ref[pair, 4:] = refs[0][2 * pair : 2 * pair + 2]


def final_kernel(source_ref, own_ref, other_ref, out_ref, sources_ref, left_ref, sum_ref):
    side = lax.axis_index("core")
    refs = ((own_ref, side), (other_ref, 1 - side))
    for k in range(2 * NS):
        for ref, at in refs:
            rows = pl.ds(pl.multiple_of(at * LANES, LANES), LANES)
            sources_ref[k, rows] = ref[k, :4].reshape(LANES, SC)
    block = 2 * WIDTH
    for pair in range(8):
        for which, (ref, at) in enumerate(refs):
            left_ref[which * 8 + pair] = ref[pair, 4 + side]
    left = left_ref[...].reshape(NC * block, NEV)
    for s in range(NS):
        for part in range(2):
            value = jnp.dot(left, sources_ref[s * 2 + part], preferred_element_type=F32)
            value = value.reshape(NC, block, SC)
            if s == 0:
                sum_ref[part] = value
                continue
            for which, (ref, at) in enumerate(refs):
                for pair in range(8):
                    row = which * 8 + pair
                    mask = source_ref[2 * pair + at] == s
                    mask = jnp.tile(mask, (block // 8, SC // LANES))
                    sum_ref[part, row] = jnp.where(mask, value[row], sum_ref[part, row])
    scale = (2.0 * NEV) ** (-0.5)
    for pair in range(8):
        for which, (ref, at) in enumerate(refs):
            e = 2 * pair + at
            by_real = sum_ref[0, which * 8 + pair]
            by_imag = sum_ref[1, which * 8 + pair]
            out_ref[e, 0] = ((by_real[:WIDTH] + by_imag[WIDTH:]) * scale).astype(BF16)
            out_ref[e, 1] = ((by_imag[:WIDTH] - by_real[WIDTH:]) * scale).astype(BF16)


def all_to_all(x, axes):
    return lax.all_to_all(x, axes, split_axis=0, concat_axis=0, tiled=True)


def spread(scatter, root):
    return pl.pallas_call(
        pick_kernel,
        in_specs=[vmem()] * 2,
        out_specs=vmem(),
        out_shape=jax.ShapeDtypeStruct((NC, WIDTH, LANES), BF16),
        compiler_params=PARAMS,
        cost_estimate=pl.CostEstimate(flops=100_000, bytes_accessed=200_000, transcendentals=0),
        name="pick",
    )(root, all_to_all(scatter, TM))


def gather(rows, order, *weighted):
    packed = pl.pallas_call(
        pack_kernel,
        in_specs=[vmem()] * (2 + len(weighted)),
        out_specs=vmem(),
        out_shape=jax.ShapeDtypeStruct((8, 4 + 2 * len(weighted), 2 * WIDTH, NEV), BF16),
        compiler_params=PARAMS,
        name="pack",
    )(order, rows, *weighted)
    own = all_to_all(packed, ("yl", "x"))
    return own, lax.ppermute(own, "core", [(0, 1), (1, 0)])


def late_sources(src):
    same = src[:, None] == src[None, :]
    earlier = jnp.arange(NS)[:, None] > jnp.arange(NS)[None, :]
    fresh = ~jnp.any(same & earlier, axis=1)
    groups = src // TD
    lower = (groups[:, None] == groups[None, :]) & (src[None, :] < src[:, None]) & fresh[None, :]
    return jnp.sum(lower.astype(jnp.int32), axis=1) >= HALF


def per_device(eigvecs, solutions, elementals, source_list, pair_owner, dilution_order):
    order = dilution_order.reshape(1, -1)
    (first,) = project(0, source_list, eigvecs, solutions)
    first, later = lax.optimization_barrier((first, source_list))
    recv = all_to_all(first, SPACE)
    kept, to_z, to_y, to_both, elems, place, root, source, slot = project(
        1, later, eigvecs, solutions, pair_owner, elementals
    )
    early, scatter = pl.pallas_call(
        reduce_kernel,
        in_specs=[vmem()] * 2,
        out_specs=[vmem()] * 2,
        out_shape=[
            jax.ShapeDtypeStruct((HALF, 2, WIDTH, NEV), BF16),
            jax.ShapeDtypeStruct((NC, WIDTH, LANES), BF16),
        ],
        compiler_params=PARAMS,
        cost_estimate=pl.CostEstimate(flops=500_000, bytes_accessed=500_000, transcendentals=0),
        name="reduce",
    )(place, recv)

    came = [
        along_z(to_z, lambda z: z ^ 1),
        lax.ppermute(to_y, "yh", [(0, 1), (1, 0)]),
        lax.ppermute(to_both, SPACE, [(c, c ^ 9) for c in range(NC)]),
    ]
    terms = pl.pallas_call(
        pair_kernel,
        in_specs=[pl.BlockSpec(memory_space=pl.ANY)] + [vmem()] * 4,
        out_specs=[vmem()] * 4,
        out_shape=[jax.ShapeDtypeStruct(BLOCK, dtype) for dtype in (F32, BF16, BF16, BF16)],
        compiler_params=PARAMS,
        cost_estimate=pl.CostEstimate(flops=500_000, bytes_accessed=500_000, transcendentals=0),
        name="pair",
    )(scatter, kept, *came)
    terms = list(terms)
    for d in range(1, NZ // 2):
        terms[d] = along_z(terms[d], lambda z: (z + 2 * d) % NZ)
    picked = spread(scatter, root)
    rows = all_to_all(picked, SPACE)
    weighted, late = pl.pallas_call(
        weigh_kernel,
        in_specs=[vmem()] * (4 + len(terms)),
        out_specs=[vmem()] * 2,
        out_shape=[
            jax.ShapeDtypeStruct((NC, 2 * WIDTH, NEV), BF16),
            jax.ShapeDtypeStruct((NC, WIDTH, LANES), BF16),
        ],
        compiler_params=PARAMS,
        cost_estimate=pl.CostEstimate(flops=70_000_000, bytes_accessed=2_000_000, transcendentals=0),
        name="weigh",
    )(slot, place, early, elems, *terms)

    own, other = gather(rows, order, weighted)

    is_late = late_sources(source_list)

    def again(own, other, late):
        own_late, other_late = gather(all_to_all(spread(late, root), SPACE), order)
        pick = jnp.repeat(is_late, 2)[:, None, None, None]
        own = own.at[:, :4].set(jnp.where(pick, own_late, own[:, :4]))
        other = other.at[:, :4].set(jnp.where(pick, other_late, other[:, :4]))
        return own, other

    own, other = lax.cond(jnp.any(is_late), again, lambda own, other, late: (own, other), own, other, late)

    return pl.pallas_call(
        final_kernel,
        in_specs=[vmem()] * 3,
        out_specs=vmem(),
        out_shape=jax.ShapeDtypeStruct((NC, 2, WIDTH, SC), BF16),
        scratch_shapes=[
            pltpu.VMEM((2 * NS, NEV, SC), BF16),
            pltpu.VMEM((NC, 2 * WIDTH, NEV), BF16),
            pltpu.VMEM((2, NC, 2 * WIDTH, SC), F32),
        ],
        compiler_params=PARAMS,
        name="final",
    )(source, own, other)


def solution(mesh):
    fine = Mesh(mesh.devices.reshape(2, 4, 2, 2, 8), TM + SPACE)
    in_specs = (
        P(None, TM, SPACE, None),
        P(None, TM, SPACE, None),
        P(None, TM, None, None),
        P(),
        P(),
        P(),
    )
    return jax.shard_map(
        per_device, mesh=fine, in_specs=in_specs, out_specs=P(TM, None, SPACE, None), check_vma=False
    )
```

```python
import functools

import jax
import jax.numpy as jnp
from jax import lax
from jax.experimental import pallas as pl
from jax.experimental.pallas import tpu as pltpu
from jax.sharding import Mesh
from jax.sharding import PartitionSpec as P

TM = ("yl", "x", "core")
SPACE = ("yh", "z")
TD = 4
HALF = 2
NZ = 8
NS = 4
NC = 16
NEV = 256
SC = 256
WIDTH = 16
SPINS = 4
LANES = 128
BLOCK = (HALF, 2, WIDTH, 256)
F32 = jnp.float32
BF16 = jnp.bfloat16
PARAMS = pltpu.CompilerParams(vmem_limit_bytes=40 * 2**20)


def smem():
    return pl.BlockSpec(memory_space=pltpu.SMEM)


def vmem():
    return pl.BlockSpec(memory_space=pltpu.VMEM)


def slot_list(src, group):
    flags = []
    for t in range(TD):
        hit = src(0) == group * TD + t
        for s in range(1, NS):
            hit = jnp.logical_or(hit, src(s) == group * TD + t)
        flags.append(hit.astype(jnp.int32))
    total = flags[0] + flags[1] + flags[2] + flags[3]
    slots = []
    before = jnp.int32(0)
    for t in range(TD):
        slots.append(jnp.where(flags[t] == 1, before, total + t - before))
        before = before + flags[t]
    return slots


def slot_of(slots, t):
    out = slots[0]
    for k in range(1, TD):
        out = jnp.where(t == k, slots[k], out)
    return out


def timeslice_at(slots, place):
    out = jnp.int32(0)
    for t in range(1, TD):
        out = jnp.where(slots[t] == place, t, out)
    return out


def my_slots(src_ref):
    return slot_list(lambda s: src_ref[s], lax.axis_index(TM))


def write_masks(src_ref, owner_ref, place_ref, root_ref, source_ref, slot_ref):
    me = lax.axis_index(TM)
    slots = my_slots(src_ref)
    full = functools.partial(jnp.full, (8, LANES), dtype=jnp.int32)
    for s in range(NS):
        place = slot_of(slots, lax.rem(src_ref[s], TD))
        for k in range(TD):
            place_ref[s * TD + k] = full((place == k).astype(jnp.int32))
    mine = lax.div(src_ref[lax.div(me, 4)], TD)
    for e in range(NC):
        root_ref[e] = full((mine == e).astype(jnp.int32))
        source = jnp.int32(0)
        for j in range(TD * NS):
            source = jnp.where(owner_ref[e, j] == me, j % NS, source)
        source_ref[e] = full(source)
    for j in range(TD * NS):
        slot_ref[owner_ref[me, j]] = full(slots[j // NS])


def project_kernel(half, src_ref, vec_hbm, sol_hbm, *refs):
    if half == 1:
        (owner_ref, elem_ref), refs = refs[:2], refs[2:]
    outs, (vec_ref, sol_ref, sems) = refs[: 1 + half * 8], refs[1 + half * 8 : 4 + half * 8]
    slots = my_slots(src_ref)
    depth = vec_ref.shape[2]
    cuts = [(0, depth)] * HALF if half else [(0, 512, depth)] + [(0, depth)] * (HALF - 1)
    copies = {}
    for k in range(HALF):
        t = timeslice_at(slots, half * HALF + k)
        for piece, (low, high) in enumerate(zip(cuts[k][:-1], cuts[k][1:])):
            rows = pl.ds(low, high - low)
            copies[k, piece] = [
                pltpu.make_async_copy(hbm.at[part, t, rows], ref.at[k, part, rows], sems.at[k, piece, part, i])
                for part in range(2)
                for i, (hbm, ref) in enumerate(((vec_hbm, vec_ref), (sol_hbm, sol_ref)))
            ]
            for copy in copies[k, piece]:
                copy.start()
    if half == 1:
        write_masks(src_ref, owner_ref, *outs[5:])
        for k in range(TD):
            for part in range(2):
                outs[4][k, part] = elem_ref[part, timeslice_at(slots, k)]
    dims = (((0,), (0,)), ((), ()))
    for k in range(HALF):
        values = [None, None]
        for piece, (low, high) in enumerate(zip(cuts[k][:-1], cuts[k][1:])):
            for copy in copies[k, piece]:
                copy.wait()
            sol = sol_ref[k, :, low:high].reshape(2 * (high - low), SC)
            vec = vec_ref[k, :, low:high]
            straight = vec.reshape(2 * (high - low), NEV)
            turned = jnp.concatenate([-vec[1], vec[0]], axis=0)
            for part, right in enumerate((straight, turned)):
                value = lax.dot_general(sol, right, dims, preferred_element_type=F32)
                values[part] = value if piece == 0 else values[part] + value
        for part, value in enumerate(values):
            if half == 0:
                outs[0][:, k, part] = value.astype(BF16).reshape(NC, WIDTH, NEV)
            else:
                value = value.reshape(2, NZ, WIDTH, NEV)
                for yh in range(2):
                    refs[-1][:, yh, k, part] = value[yh]
    if half == 1:
        parity = lax.rem(lax.axis_index("z"), 2)
        yh = lax.axis_index("yh")
        for k in range(NZ // 2):
            same, other = 2 * k + parity, 2 * k + 1 - parity
            outs[0][k] = refs[-1][same, yh]
            outs[1][k] = refs[-1][other, yh].astype(BF16)
            outs[2][k] = refs[-1][same, 1 - yh].astype(BF16)
            outs[3][k] = refs[-1][other, 1 - yh].astype(BF16)


def project(half, src, eigvecs, solutions, *more):
    depth = eigvecs.shape[2]
    scratch = [
        pltpu.VMEM((HALF, 2, depth, NEV), BF16),
        pltpu.VMEM((HALF, 2, depth, SC), BF16),
        pltpu.SemaphoreType.DMA((HALF, 2, 2, 2)),
    ]
    if half == 0:
        shapes = [jax.ShapeDtypeStruct((NC, HALF, 2, WIDTH, NEV), BF16)]
    else:
        shapes = [jax.ShapeDtypeStruct((NZ // 2,) + BLOCK, dtype) for dtype in (F32, BF16, BF16, BF16)]
        shapes.append(jax.ShapeDtypeStruct((TD, 2, NEV, NEV), BF16))
        shapes += [jax.ShapeDtypeStruct((NC, 8, LANES), jnp.int32)] * 4
        scratch.append(pltpu.VMEM((NZ, 2) + BLOCK, F32))
    return pl.pallas_call(
        functools.partial(project_kernel, half),
        in_specs=[smem()] + [pl.BlockSpec(memory_space=pl.ANY)] * 2 + [smem(), vmem()][: len(more)],
        out_specs=[vmem()] * len(shapes),
        out_shape=shapes,
        scratch_shapes=scratch,
        compiler_params=pltpu.CompilerParams(vmem_limit_bytes=(58, 50)[half] * 2**20),
        cost_estimate=pl.CostEstimate(flops=1_400_000_000, bytes_accessed=6_000_000, transcendentals=0),
        name="project%d" % half,
    )(src, eigvecs, solutions, *more)


def scatter_sources(place_ref, half, totals, scatter_ref):
    for s in range(NS):
        for part in range(2):
            for side in range(2):
                lanes = slice(side * LANES, (side + 1) * LANES)
                rows = totals[0][part, :, lanes]
                for k in range(1, HALF):
                    mask = place_ref[s * TD + half * HALF + k]
                    rows = jnp.where(jnp.concatenate([mask, mask]) != 0, totals[k][part, :, lanes], rows)
                scatter_ref[(s * 2 + part) * 2 + side] = rows.astype(BF16)


def reduce_kernel(place_ref, recv_ref, total_ref, scatter_ref):
    totals = []
    for k in range(HALF):
        total = recv_ref[0, k].astype(F32)
        for c in range(1, NC):
            total = total + recv_ref[c, k].astype(F32)
        total_ref[k] = total.astype(BF16)
        totals.append(total)
    scatter_sources(place_ref, 0, totals, scatter_ref)


def pair_kernel(after_ref, kept_ref, *refs):
    del after_ref
    came_refs, own_ref, send_refs = refs[:3], refs[3], refs[4:]
    half = lax.div(lax.axis_index("z"), 2)
    for d in range(NZ // 2):
        at = lax.rem(half + d, NZ // 2)
        total = kept_ref[at]
        for ref in came_refs:
            total = total + ref[at].astype(F32)
        if d == 0:
            own_ref[...] = total
        else:
            send_refs[d - 1][...] = total.astype(BF16)


def along_z(x, to):
    return lax.ppermute(x, "z", [(z, to(z)) for z in range(NZ)])


def weigh_kernel(slot_ref, place_ref, early_ref, elem_ref, *refs):
    terms, (out_ref, late_ref) = refs[:-2], refs[-2:]
    totals = []
    for k in range(HALF):
        total = terms[0][k]
        for term in terms[1:]:
            total = total + term[k].astype(F32)
        totals.append(total)
    weighted = []
    for k in range(TD):
        both = early_ref[k] if k < HALF else totals[k - HALF].astype(BF16)
        both = both.reshape(2 * WIDTH, NEV)
        by_real = jnp.dot(both, elem_ref[k, 0], preferred_element_type=F32)
        by_imag = jnp.dot(both, elem_ref[k, 1], preferred_element_type=F32)
        real = by_real[:WIDTH] + by_imag[WIDTH:]
        imag = by_real[WIDTH:] - by_imag[:WIDTH]
        weighted.append(jnp.concatenate([real, imag], axis=0))
    for d in range(NC):
        slot = jnp.tile(slot_ref[d], (2 * WIDTH // 8, NEV // LANES))
        value = weighted[0]
        for k in range(1, TD):
            value = jnp.where(slot == k, weighted[k], value)
        out_ref[d] = value.astype(BF16)
    scatter_sources(place_ref, 1, totals, late_ref)


def pick_kernel(root_ref, parts_ref, out_ref):
    part = parts_ref[0].astype(F32)
    for e in range(1, NC):
        mask = root_ref[e]
        part = jnp.where(jnp.concatenate([mask, mask]) != 0, parts_ref[e].astype(F32), part)
    part = part.astype(BF16)
    for c in range(NC):
        out_ref[c] = part


def pack_kernel(order_ref, rows_ref, *refs):
    out_ref = refs[-1]
    order = order_ref[...]
    wide = jnp.concatenate([order + spin * (SC // SPINS) for spin in range(SPINS)], axis=1)
    chosen = (lax.broadcasted_iota(jnp.int32, (SC, SC), 0) == wide).astype(BF16)
    rows = rows_ref[...].reshape(SC, LANES)
    dims = (((0,), (0,)), ((), ()))
    part = lax.dot_general(rows, chosen, dims, preferred_element_type=F32).astype(BF16)
    part = part.reshape(4, 2 * WIDTH, SC)
    for pair in range(8):
        out_ref[pair, :4] = part
        if len(refs) > 1:
            out_ref[pair, 4:] = refs[0][2 * pair : 2 * pair + 2]


def final_kernel(source_ref, own_ref, other_ref, out_ref, sources_ref, left_ref, sum_ref):
    side = lax.axis_index("core")
    refs = ((own_ref, side), (other_ref, 1 - side))
    for k in range(2 * NS):
        for ref, at in refs:
            rows = pl.ds(pl.multiple_of(at * LANES, LANES), LANES)
            sources_ref[k, rows] = ref[k, :4].reshape(LANES, SC)
    block = 2 * WIDTH
    for pair in range(8):
        for which, (ref, at) in enumerate(refs):
            left_ref[which * 8 + pair] = ref[pair, 4 + side]
    left = left_ref[...].reshape(NC * block, NEV)
    for s in range(NS):
        for part in range(2):
            value = jnp.dot(left, sources_ref[s * 2 + part], preferred_element_type=F32)
            value = value.reshape(NC, block, SC)
            if s == 0:
                sum_ref[part] = value
                continue
            for which, (ref, at) in enumerate(refs):
                for pair in range(8):
                    row = which * 8 + pair
                    mask = source_ref[2 * pair + at] == s
                    mask = jnp.tile(mask, (block // 8, SC // LANES))
                    sum_ref[part, row] = jnp.where(mask, value[row], sum_ref[part, row])
    scale = (2.0 * NEV) ** (-0.5)
    for pair in range(8):
        for which, (ref, at) in enumerate(refs):
            e = 2 * pair + at
            by_real = sum_ref[0, which * 8 + pair]
            by_imag = sum_ref[1, which * 8 + pair]
            out_ref[e, 0] = ((by_real[:WIDTH] + by_imag[WIDTH:]) * scale).astype(BF16)
            out_ref[e, 1] = ((by_imag[:WIDTH] - by_real[WIDTH:]) * scale).astype(BF16)


def all_to_all(x, axes):
    return lax.all_to_all(x, axes, split_axis=0, concat_axis=0, tiled=True)


def spread(scatter, root):
    return pl.pallas_call(
        pick_kernel,
        in_specs=[vmem()] * 2,
        out_specs=vmem(),
        out_shape=jax.ShapeDtypeStruct((NC, WIDTH, LANES), BF16),
        compiler_params=PARAMS,
        cost_estimate=pl.CostEstimate(flops=100_000, bytes_accessed=200_000, transcendentals=0),
        name="pick",
    )(root, all_to_all(scatter, TM))


def gather(rows, order, *weighted):
    packed = pl.pallas_call(
        pack_kernel,
        in_specs=[vmem()] * (2 + len(weighted)),
        out_specs=vmem(),
        out_shape=jax.ShapeDtypeStruct((8, 4 + 2 * len(weighted), 2 * WIDTH, NEV), BF16),
        compiler_params=PARAMS,
        name="pack",
    )(order, rows, *weighted)
    own = all_to_all(packed, ("yl", "x"))
    return own, lax.ppermute(own, "core", [(0, 1), (1, 0)])


def late_sources(src):
    same = src[:, None] == src[None, :]
    earlier = jnp.arange(NS)[:, None] > jnp.arange(NS)[None, :]
    fresh = ~jnp.any(same & earlier, axis=1)
    groups = src // TD
    lower = (groups[:, None] == groups[None, :]) & (src[None, :] < src[:, None]) & fresh[None, :]
    return jnp.sum(lower.astype(jnp.int32), axis=1) >= HALF


def per_device(eigvecs, solutions, elementals, source_list, pair_owner, dilution_order):
    order = dilution_order.reshape(1, -1)
    (first,) = project(0, source_list, eigvecs, solutions)
    first, later = lax.optimization_barrier((first, source_list))
    recv = all_to_all(first, SPACE)
    kept, to_z, to_y, to_both, elems, place, root, source, slot = project(
        1, later, eigvecs, solutions, pair_owner, elementals
    )
    early, scatter = pl.pallas_call(
        reduce_kernel,
        in_specs=[vmem()] * 2,
        out_specs=[vmem()] * 2,
        out_shape=[
            jax.ShapeDtypeStruct((HALF, 2, WIDTH, NEV), BF16),
            jax.ShapeDtypeStruct((NC, WIDTH, LANES), BF16),
        ],
        compiler_params=PARAMS,
        cost_estimate=pl.CostEstimate(flops=500_000, bytes_accessed=500_000, transcendentals=0),
        name="reduce",
    )(place, recv)

    came = [
        along_z(to_z, lambda z: z ^ 1),
        lax.ppermute(to_y, "yh", [(0, 1), (1, 0)]),
        lax.ppermute(to_both, SPACE, [(c, c ^ 9) for c in range(NC)]),
    ]
    terms = pl.pallas_call(
        pair_kernel,
        in_specs=[pl.BlockSpec(memory_space=pl.ANY)] + [vmem()] * 4,
        out_specs=[vmem()] * 4,
        out_shape=[jax.ShapeDtypeStruct(BLOCK, dtype) for dtype in (F32, BF16, BF16, BF16)],
        compiler_params=PARAMS,
        cost_estimate=pl.CostEstimate(flops=500_000, bytes_accessed=500_000, transcendentals=0),
        name="pair",
    )(scatter, kept, *came)
    terms = list(terms)
    for d in range(1, NZ // 2):
        terms[d] = along_z(terms[d], lambda z: (z + 2 * d) % NZ)
    picked = spread(scatter, root)
    rows = all_to_all(picked, SPACE)
    weighted, late = pl.pallas_call(
        weigh_kernel,
        in_specs=[vmem()] * (4 + len(terms)),
        out_specs=[vmem()] * 2,
        out_shape=[
            jax.ShapeDtypeStruct((NC, 2 * WIDTH, NEV), BF16),
            jax.ShapeDtypeStruct((NC, WIDTH, LANES), BF16),
        ],
        compiler_params=PARAMS,
        cost_estimate=pl.CostEstimate(flops=70_000_000, bytes_accessed=2_000_000, transcendentals=0),
        name="weigh",
    )(slot, place, early, elems, *terms)

    own, other = gather(rows, order, weighted)

    is_late = late_sources(source_list)

    def again(own, other, late):
        own_late, other_late = gather(all_to_all(spread(late, root), SPACE), order)
        pick = jnp.repeat(is_late, 2)[:, None, None, None]
        own = own.at[:, :4].set(jnp.where(pick, own_late, own[:, :4]))
        other = other.at[:, :4].set(jnp.where(pick, other_late, other[:, :4]))
        return own, other

    own, other = lax.cond(jnp.any(is_late), again, lambda own, other, late: (own, other), own, other, late)

    return pl.pallas_call(
        final_kernel,
        in_specs=[vmem()] * 3,
        out_specs=vmem(),
        out_shape=jax.ShapeDtypeStruct((NC, 2, WIDTH, SC), BF16),
        scratch_shapes=[
            pltpu.VMEM((2 * NS, NEV, SC), BF16),
            pltpu.VMEM((NC, 2 * WIDTH, NEV), BF16),
            pltpu.VMEM((2, NC, 2 * WIDTH, SC), F32),
        ],
        compiler_params=PARAMS,
        name="final",
    )(source, own, other)


def solution(mesh):
    fine = Mesh(mesh.devices.reshape(2, 4, 2, 2, 8), TM + SPACE)
    in_specs = (
        P(None, TM, SPACE, None),
        P(None, TM, SPACE, None),
        P(None, TM, None, None),
        P(),
        P(),
        P(),
    )
    return jax.shard_map(
        per_device, mesh=fine, in_specs=in_specs, out_specs=P(TM, None, SPACE, None), check_vma=False
    )
```
